32 devices in a mesh: mem: 2 (over x), reg: 16 (over z, y, core).
Axes of the slice: x: 2, y: 2, z: 4, core: 2. Of those that a mesh axis runs over, the one named last changes fastest.
Arguments:
- members: bfloat16 [512, 256, 128], P('mem', 'reg'), may hold values from -6 to 6
- diffusivity: float32 [256, 128], P('reg'), may hold values from 0.02 to 0.2
- advection: float32 [256, 128], P('reg'), may hold values from -0.3 to 0.3
- obs_value: bfloat16 [16, 2, 256], P('reg', 'mem'), may hold values from -6 to 6
- obs_rinv: float32 [16, 2, 256], P('reg', 'mem'), may hold values from 0.5 to 4
- obs_cell: int32 [16, 2, 256], P('reg', 'mem'), may hold values from 0 to 1023
- obs_count: int32 [16, 2], P('reg', 'mem'), may hold values from 64 to 256, as said below
- loc_index: int32 [16, 2, 256], P('reg', 'mem'), may hold values from 0 to 7
Outputs:
- analysis: float32 [512, 256, 128], P('mem', 'reg')
The draws below stay inside these ranges and needn't reach their ends.
Inputs may be any that keep to these rules, and one draw needn't show every extreme that they name: `obs_count`: each patch has 64 to 256 live slots, and some patch has exactly 256.
All inputs are finite; a program needn't handle non-finite values.
Results may differ from the reference program's by a relative error of at most 0.0047.
Values may be sent and summed in bfloat16 or wider, within the bound.
A program may use at most 64 MiB of HBM per device.

```python
import math
import jax
import jax.numpy as jnp
from jax import lax

ENSEMBLE_SIZE = 512
TILE_LINES = 8
LATTICE_BREADTH = 128
OWN = 256
STEPS = 3
NSIT = 2
ZONE_TOTAL = 16
GRID_ROWS = 256
N_MEM = 2


def draw_obs_count(key, part):
    first_key, second_key = jax.random.split(jax.random.fold_in(key, 7))
    counts = jax.random.randint(first_key, (ZONE_TOTAL * N_MEM,), OWN // 4, OWN + 1, dtype=jnp.int32)
    chosen = jax.random.randint(second_key, (), 0, ZONE_TOTAL * N_MEM, dtype=jnp.int32)
    counts = jnp.where(jnp.arange(ZONE_TOTAL * N_MEM, dtype=jnp.int32) == chosen, OWN, counts)
    return counts.reshape(ZONE_TOTAL, N_MEM)


def plant(array, own_key, smallest, high):
    longest = array.shape.index(max(array.shape))
    spots = []
    for shift in (0, 1):
        where = [jax.random.randint(jax.random.fold_in(own_key, axis), (), 0, length) for axis, length in enumerate(array.shape)]
        where[longest] = (where[longest] + shift) % array.shape[longest]
        spots.append(tuple(where))
    return array.at[spots[0]].set(smallest).at[spots[1]].set(high)


def steps_of(key, shape, shards, low, top_value):
    level = 1.0
    for axis_at, parts in shards:
        heights = jax.random.uniform(jax.random.fold_in(jax.random.fold_in(key, 6), axis_at), (parts,), jnp.float32, low / len(shards), top_value / len(shards))
        level = level * jnp.repeat(jnp.exp(heights), shape[axis_at] // parts).reshape((-1,) + (1,) * (len(shape) - 1 - axis_at))
    return level


def noise(own_key, dims, scale, most, pieces=(), held_as=jnp.bfloat16):
    loudness = steps_of(own_key, dims, pieces, -0.22, 0.18) if pieces else 1.0
    values = jax.random.normal(own_key, dims, jnp.float32) * scale * loudness
    return jnp.minimum(jnp.maximum(values, -most), most).astype(held_as)


def setup_inputs(seed: int = 0) -> dict:
    key_of = jax.random.split(jax.random.key(seed), 9)
    return {
        "members": noise(key_of[0], (ENSEMBLE_SIZE, GRID_ROWS, LATTICE_BREADTH), 1.0, 6.0, ((0, 2), (1, 16))),
        "diffusivity": jnp.clip(jnp.exp(math.log(0.2) - 2.3025851 * jax.random.uniform(key_of[1], (GRID_ROWS, LATTICE_BREADTH), jnp.float32) ** steps_of(key_of[1], (GRID_ROWS, LATTICE_BREADTH), ((0, 16),), -0.2, 0.2)), 0.02, 0.2),
        "advection": jnp.clip(jax.random.uniform(key_of[2], (GRID_ROWS, LATTICE_BREADTH), jnp.float32, -0.3, 0.3) * steps_of(key_of[2], (GRID_ROWS, LATTICE_BREADTH), ((0, 16),), -0.4, 0.0), -0.3, 0.3),
        "obs_value": noise(key_of[3], (ZONE_TOTAL, N_MEM, OWN), 1.0, 6.0, ((0, 16), (1, 2))),
        "obs_rinv": jnp.clip(jnp.exp(math.log(4.0) - 2.0794415 * jax.random.uniform(key_of[4], (ZONE_TOTAL, N_MEM, OWN), jnp.float32) ** steps_of(key_of[4], (ZONE_TOTAL, N_MEM, OWN), ((0, 16), (1, 2)), -0.2, 0.2)), 0.5, 4.0),
        "obs_cell": plant(jax.random.randint(key_of[5], (ZONE_TOTAL, N_MEM, OWN), 0, TILE_LINES * LATTICE_BREADTH), jax.random.fold_in(key_of[5], 1), 0, (TILE_LINES * LATTICE_BREADTH) - 1).astype(jnp.int32),
        "obs_count": draw_obs_count(jax.random.fold_in(key_of[8], 71), 0),
        "loc_index": plant(jax.random.randint(key_of[7], (ZONE_TOTAL, N_MEM, OWN), 0, 8), jax.random.fold_in(key_of[7], 1), 0, 7).astype(jnp.int32),
    }


def advance_all(ensemble_sample_array, diffusivity, advection):
    north_row = jnp.roll(ensemble_sample_array, 1, 1)
    south_row = jnp.roll(ensemble_sample_array, -1, 1)
    east_cell = jnp.roll(ensemble_sample_array, -1, 2)
    west_cell = jnp.roll(ensemble_sample_array, 1, 2)
    return ensemble_sample_array + diffusivity * (north_row + south_row + east_cell + west_cell - 4.0 * ensemble_sample_array) - advection * 0.5 * (south_row - north_row)

def analyse(states, ens_obs, value_all, prec_all):
    members_count = states.shape[0]
    identity = jnp.eye(members_count, dtype=jnp.float32)
    obs_float = ens_obs.astype(jnp.float32)
    obs_mean = lax.optimization_barrier(jnp.mean(obs_float, axis=0))
    obs_perturb = obs_float - obs_mean[None, :]
    innovation = value_all - obs_mean
    weighted = obs_perturb * prec_all[None, :]
    system = jnp.dot(weighted, obs_perturb.T, precision=lax.Precision.HIGHEST) + (members_count - 1.0) * identity
    forcing = jnp.dot(weighted, innovation, precision=lax.Precision.HIGHEST)
    scale_value = jnp.sqrt(jnp.sum(system * system))
    root_iter = system / scale_value
    inverse_root = identity
    for sweep in range(NSIT):
        correction = 1.5 * identity - 0.5 * jnp.dot(inverse_root, root_iter, precision=lax.Precision.HIGHEST)
        root_iter = jnp.dot(root_iter, correction, precision=lax.Precision.HIGHEST)
        inverse_root = jnp.dot(correction, inverse_root, precision=lax.Precision.HIGHEST)
    mean_weights = jnp.dot(inverse_root, jnp.dot(inverse_root, forcing, precision=lax.Precision.HIGHEST), precision=lax.Precision.HIGHEST) / scale_value
    transform = (jnp.sqrt((members_count - 1.0) / scale_value) * inverse_root + mean_weights[:, None]).astype(jnp.bfloat16)
    state_float = states.astype(jnp.float32)
    state_mean = lax.optimization_barrier(jnp.mean(state_float, axis=0))
    state_perturb = (state_float - state_mean[None, :]).astype(jnp.bfloat16)
    return state_mean[None, :] + jnp.dot(transform.T, state_perturb, preferred_element_type=jnp.float32)

def reference(members, diffusivity, advection, obs_value, obs_rinv, obs_cell, obs_count, loc_index):
    ensemble_sample_array = members.astype(jnp.float32)
    for sweep in range(STEPS):
        ensemble_sample_array = advance_all(ensemble_sample_array, diffusivity, advection)
    propagate_ensemble = ensemble_sample_array.astype(jnp.bfloat16)
    tile_variables = propagate_ensemble.reshape(ENSEMBLE_SIZE, ZONE_TOTAL, N_MEM, TILE_LINES * LATTICE_BREADTH).transpose(1, 2, 0, 3)
    obs_space = jax.vmap(jax.vmap(lambda states, cells: jnp.take(states, cells, axis=1)))(tile_variables, obs_cell)
    slot_index = jnp.arange(OWN, dtype=jnp.int32)
    live_slot = (slot_index[None, None, :] < obs_count[:, :, None]).astype(jnp.float32)
    own_prec = obs_rinv * live_slot
    loc_float = loc_index.astype(jnp.float32)
    far_prec = (own_prec * jnp.exp(-((loc_float + 1.0) / 4.0) ** 2)).astype(jnp.bfloat16)

    def one_patch(patch_index):
        region = patch_index // N_MEM
        group = patch_index % N_MEM
        before = (region + ZONE_TOTAL - 1) % ZONE_TOTAL
        after = (region + 1) % ZONE_TOTAL
        ens_obs = jnp.concatenate([obs_space[region, group], obs_space[before, group], obs_space[after, group]], axis=1)
        value_all = jnp.concatenate([obs_value[region, group], obs_value[before, group], obs_value[after, group]]).astype(jnp.float32)
        prec_all = jnp.concatenate([own_prec[region, group], far_prec[before, group].astype(jnp.float32), far_prec[after, group].astype(jnp.float32)])
        return analyse(tile_variables[region, group], ens_obs, value_all, prec_all)
    results = lax.map(one_patch, jnp.arange(ZONE_TOTAL * N_MEM, dtype=jnp.int32))
    results = results.reshape(ZONE_TOTAL, N_MEM, ENSEMBLE_SIZE, TILE_LINES, LATTICE_BREADTH).transpose(2, 0, 1, 3, 4)
    return results.reshape(ENSEMBLE_SIZE, GRID_ROWS, LATTICE_BREADTH)
```

```python
import functools

import jax
import jax.numpy as jnp
from jax import lax
from jax.experimental import pallas as pl
from jax.experimental.pallas import tpu as pltpu
from jax.sharding import PartitionSpec as P

STEPS = 3
MESH = pl.DeviceIdType.MESH
F32 = jnp.float32
BF16 = jnp.bfloat16
MEMBER_BLOCK = 64


def kernel(
    groups, regions,
    mem_ref, dif_ref, adv_ref, val_ref, rinv_ref, cell_ref, cnt_ref, loc_ref,
    out_ref,
    padded, first, second, fc, states, coef, coef_in, cells_out, cells_in,
    info_out, info_in, hsend, hall, wt, xb, xbar, ret_out, ret_in,
    local_sem, send_sem, recv_sem,
):
    lines, local, width = mem_ref.shape
    patch = lines // groups
    slots = hall.shape[2]
    members = groups * local
    halo = STEPS
    m = lax.axis_index("mem")
    r = lax.axis_index("reg")
    up = lax.rem(r + regions - 1, regions)
    down = lax.rem(r + 1, regions)

    barrier = pltpu.get_barrier_semaphore()
    for side in (up, down):
        pl.semaphore_signal(barrier, inc=1, device_id=(m, side), device_id_type=MESH)
    for j in range(1, groups):
        pl.semaphore_signal(barrier, inc=1, device_id=(lax.rem(m + j, groups), r), device_id_type=MESH)
    own_load = pltpu.make_async_copy(mem_ref, padded.at[pl.ds(halo, lines)], local_sem.at[0])
    own_load.start()
    cells_out[...] = jnp.broadcast_to(cell_ref[0], cells_out.shape)
    slot = lax.broadcasted_iota(jnp.int32, (1, slots), 1)
    own_prec = jnp.where(slot < cnt_ref[...], rinv_ref[0], 0.0)
    reach = (loc_ref[0].astype(F32) + 1.0) * 0.25
    far_prec = (own_prec * jnp.exp(-(reach * reach))).astype(BF16).astype(F32)
    own_val = val_ref[0].astype(F32)
    info_row = lax.broadcasted_iota(jnp.int32, info_out.shape, 0)
    info_out[...] = jnp.where(info_row == 0, own_val, far_prec)
    pl.semaphore_wait(barrier, groups + 1)

    copies = []

    def send(src, dst, target):
        at = len(copies)
        copy = pltpu.make_async_remote_copy(
            src_ref=src, dst_ref=dst, send_sem=send_sem.at[at], recv_sem=recv_sem.at[at],
            device_id=target, device_id_type=MESH,
        )
        copy.start()
        copies.append(copy)
        return copy

    above, below = (m, up), (m, down)
    halo_top = send(mem_ref.at[pl.ds(lines - halo, halo)], padded.at[pl.ds(0, halo)], below)
    halo_bottom = send(mem_ref.at[pl.ds(0, halo)], padded.at[pl.ds(lines + halo, halo)], above)
    coef_top = [
        send(ref.at[pl.ds(lines - 8, 8)], coef_in.at[0, i], below)
        for i, ref in enumerate((dif_ref, adv_ref))
    ]
    coef_bottom = [
        send(ref.at[pl.ds(0, 8)], coef_in.at[1, i], above)
        for i, ref in enumerate((dif_ref, adv_ref))
    ]
    cell_copies = [
        send(cells_out, cells_in.at[j - 1], (lax.rem(m + j, groups), r)) for j in range(1, groups)
    ]
    info_copies = [
        send(info_out, info_in.at[0], below),
        send(info_out, info_in.at[1], above),
    ]

    def put_coef(base, d, a):
        rows = pl.ds(base, d.shape[0])
        coef[0, rows] = 1.0 - 4.0 * d
        coef[1, rows] = d + 0.5 * a
        coef[2, rows] = d - 0.5 * a
        coef[3, rows] = d

    put_coef(8, dif_ref[...], adv_ref[...])

    def step(src, dst, shift, low, high):
        def body(p, _):
            k = [coef[i, pl.ds(p + 8 - halo, 1), :] for i in range(4)]
            for at in range(0, local, MEMBER_BLOCK):
                block = pl.ds(at, MEMBER_BLOCK)
                c = src[p, block, :].astype(F32)
                n = src[p - 1, block, :].astype(F32)
                s = src[p + 1, block, :].astype(F32)
                sides = pltpu.roll(c, width - 1, 1) + pltpu.roll(c, 1, 1)
                value = k[0] * c + k[1] * n + k[2] * s + k[3] * sides
                dst[p - shift, block, :] = value.astype(dst.dtype)
            return 0

        lax.fori_loop(low, high, body, 0)

    own_load.wait()
    step(padded, first, 0, 4, lines + 2)
    step(first, second, 0, 5, lines + 1)
    step(second, fc, halo, 6, lines)

    def forward(early):
        made = []
        for j in range(1, groups):
            g = lax.rem(m + j, groups)
            inner = (g + groups - 1) // groups
            if early:
                at, count = halo * (1 - inner), patch - halo
            else:
                at, count = (patch - halo) * inner, halo
            made.append(send(
                fc.at[pl.ds(g * patch + at, count)],
                states.at[pl.ds(at, count), pl.ds(m * local, local)],
                (g, r),
            ))
        return made

    forwards = forward(True)

    halo_top.wait_recv()
    for copy in coef_top:
        copy.wait_recv()
    put_coef(0, coef_in[0, 0], coef_in[0, 1])
    step(padded, first, 0, 1, 4)
    step(first, second, 0, 2, 5)
    step(second, fc, halo, 3, 6)
    halo_bottom.wait_recv()
    for copy in coef_bottom:
        copy.wait_recv()
    put_coef(lines + 8, coef_in[1, 0], coef_in[1, 1])
    step(padded, first, 0, lines + 2, lines + 5)
    step(first, second, 0, lines + 1, lines + 4)
    step(second, fc, halo, lines, lines + 3)

    cell_index = lax.broadcasted_iota(jnp.int32, (patch * width, slots), 0)

    def observe(g, cells):
        flat = jnp.concatenate([fc[g * patch + l] for l in range(patch)], axis=1)
        pick = jnp.where(cell_index == cells, 1.0, 0.0).astype(BF16)
        return jnp.dot(flat, pick, preferred_element_type=F32).astype(BF16)

    hx = []
    for j in range(1, groups):
        g = lax.rem(m + groups - j, groups)
        cell_copies[j - 1].wait_recv()
        hsend[j - 1] = observe(g, cells_in[j - 1, 0:1, :])
        hx.append(send(hsend.at[j - 1], hall.at[0, pl.ds(m * local, local)], (g, r)))
    forwards += forward(False)
    own_rows = pl.ds(pl.multiple_of(m * local, local), local)
    hall[0, own_rows, :] = observe(m, cell_ref[0])

    def relay(block):
        rows = pl.ds(block * local, local)
        return [
            send(hall.at[0, rows], hall.at[1, rows], below),
            send(hall.at[0, rows], hall.at[2, rows], above),
        ]

    relays = relay(m)
    for l in range(patch):
        states[l, own_rows, :] = fc[m * patch + l]
    for j in range(1, groups):
        hx[j - 1].wait_recv()
        relays += relay(lax.rem(m + j, groups))

    row_id = lax.broadcasted_iota(jnp.int32, (members, members), 0)
    col_id = lax.broadcasted_iota(jnp.int32, (members, members), 1)
    eye = jnp.where(row_id == col_id, 1.0, 0.0)

    def gram(h, value, prec):
        h = h.astype(F32)
        hbar = jnp.sum(h, axis=0, keepdims=True) * (1.0 / members)
        y = h - hbar
        weighted = y * prec
        part = lax.dot_general(
            weighted.astype(BF16), y.astype(BF16), (((1,), (1,)), ((), ())),
            preferred_element_type=F32,
        )
        return part, jnp.sum(weighted * (value - hbar), axis=1, keepdims=True)

    system, force = gram(hall[0], own_val, own_prec)
    system = system + (members - 1.0) * eye
    for copy in info_copies + relays:
        copy.wait_recv()
    for side in range(2):
        part, more = gram(hall[1 + side], info_in[side, 0:1, :], info_in[side, 1:2, :])
        system, force = system + part, force + more
    total = jnp.sum(jnp.sum(system * system, axis=0, keepdims=True), axis=1, keepdims=True)
    inv_scale = lax.rsqrt(total)
    y1 = system * inv_scale
    y1b = y1.astype(BF16)
    y2 = jnp.dot(y1b, y1b, preferred_element_type=F32)
    tail = (0.0625 * y2 - 0.5625 * y1).astype(BF16)
    z = 2.25 * eye - 2.4375 * y1 + 1.6875 * y2 + jnp.dot(
        y2.astype(BF16), tail, preferred_element_type=F32
    )
    half = jnp.sum(z * force, axis=0, keepdims=True)
    mean_col = jnp.sum(z * half, axis=1, keepdims=True) * inv_scale
    mean_row = jnp.sum(eye * mean_col, axis=0, keepdims=True)
    wt[...] = (jnp.sqrt((members - 1.0) * inv_scale) * z + mean_row).astype(BF16)

    for copy in forwards:
        copy.wait_recv()
    for l in range(patch):
        lane = pl.ds(l * width, width)
        x = states[l].astype(F32)
        mean = jnp.sum(x, axis=0, keepdims=True) * (1.0 / members)
        xbar[0:1, lane] = mean
        xb[:, lane] = (x - mean).astype(BF16)

    def result(g, l, count):
        lane = pl.ds(l * width, count * width)
        rows = pl.ds(pl.multiple_of(g * local, local), local)
        return xbar[0:1, lane] + jnp.dot(wt[rows, :], xb[:, lane], preferred_element_type=F32)

    pair = 2
    returns = []
    for l in range(0, patch, pair):
        for j in range(1, groups):
            g = lax.rem(m + j, groups)
            value = result(g, l, pair).astype(BF16)
            for i in range(pair):
                ret_out[j - 1, l + i] = value[:, i * width:(i + 1) * width]
            rows = pl.ds(l, pair)
            returns.append((j, l, send(ret_out.at[j - 1, rows], ret_in.at[j - 1, rows], (g, r))))
    for l in range(0, patch, pair):
        value = result(m, l, pair)
        for i in range(pair):
            out_ref[m * patch + l + i] = value[:, i * width:(i + 1) * width]
    for j, l, copy in returns:
        copy.wait_recv()
        g = lax.rem(m + groups - j, groups)
        for i in range(pair):
            out_ref[g * patch + l + i] = ret_in[j - 1, l + i].astype(F32)
    for copy in copies:
        copy.wait_send()


def on_device(groups, regions, members, diffusivity, advection, obs_value, obs_rinv, obs_cell, obs_count, loc_index):
    local, lines, width = members.shape
    slots = obs_cell.shape[-1]
    patch = lines // groups
    total = groups * local
    partners = groups - 1
    pairs = patch // 2
    count = 8 + partners + 2 * partners + partners + 2 * groups + partners * pairs
    vmem = pl.BlockSpec(memory_space=pltpu.VMEM)
    flops = 2 * total * total * (3 * slots + 2 * total + patch * width)
    result = pl.pallas_call(
        functools.partial(kernel, groups, regions),
        out_shape=jax.ShapeDtypeStruct((lines, local, width), F32),
        in_specs=[pl.BlockSpec(memory_space=pl.ANY)] + [vmem] * 7,
        out_specs=vmem,
        scratch_shapes=[
            pltpu.VMEM((lines + 2 * STEPS, local, width), BF16),
            pltpu.VMEM((lines + 2 * STEPS, local, width), F32),
            pltpu.VMEM((lines + 2 * STEPS, local, width), F32),
            pltpu.VMEM((lines, local, width), BF16),
            pltpu.VMEM((patch, total, width), BF16),
            pltpu.VMEM((4, lines + 16, width), F32),
            pltpu.VMEM((2, 2, 8, width), F32),
            pltpu.VMEM((8, slots), jnp.int32),
            pltpu.VMEM((partners, 8, slots), jnp.int32),
            pltpu.VMEM((8, slots), F32),
            pltpu.VMEM((2, 8, slots), F32),
            pltpu.VMEM((partners, local, slots), BF16),
            pltpu.VMEM((3, total, slots), BF16),
            pltpu.VMEM((total, total), BF16),
            pltpu.VMEM((total, patch * width), BF16),
            pltpu.VMEM((8, patch * width), F32),
            pltpu.VMEM((partners, patch, local, width), BF16),
            pltpu.VMEM((partners, patch, local, width), BF16),
            pltpu.SemaphoreType.DMA((1,)),
            pltpu.SemaphoreType.DMA((count,)),
            pltpu.SemaphoreType.DMA((count,)),
        ],
        compiler_params=pltpu.CompilerParams(
            collective_id=0, has_side_effects=True, vmem_limit_bytes=48 * 1024 * 1024
        ),
        cost_estimate=pl.CostEstimate(flops=flops, bytes_accessed=6 * lines * local * width, transcendentals=0),
    )(
        jnp.transpose(members, (1, 0, 2)), diffusivity, advection, obs_value, obs_rinv,
        obs_cell, obs_count, loc_index,
    )
    return jnp.transpose(result, (1, 0, 2))


def solution(mesh):
    return jax.shard_map(
        functools.partial(on_device, mesh.shape["mem"], mesh.shape["reg"]),
        mesh=mesh,
        in_specs=(
            P("mem", "reg", None),
            P("reg", None),
            P("reg", None),
            P("reg", "mem", None),
            P("reg", "mem", None),
            P("reg", "mem", None),
            P("reg", "mem"),
            P("reg", "mem", None),
        ),
        out_specs=P("mem", "reg", None),
        check_vma=False,
    )
```

```python
import functools

import jax
import jax.numpy as jnp
from jax import lax
from jax.experimental import pallas as pl
from jax.experimental.pallas import tpu as pltpu
from jax.sharding import PartitionSpec as P

STEPS = 3
MESH = pl.DeviceIdType.MESH
F32 = jnp.float32
BF16 = jnp.bfloat16
MEMBER_BLOCK = 64


def kernel(
    groups, regions,
    mem_ref, dif_ref, adv_ref, val_ref, rinv_ref, cell_ref, cnt_ref, loc_ref,
    out_ref,
    padded, first, second, fc, states, coef, coef_in, cells_out, cells_in,
    info_out, info_in, hsend, hall, wt, xb, xbar, ret_out, ret_in,
    local_sem, send_sem, recv_sem,
):
    lines, local, width = mem_ref.shape
    patch = lines // groups
    slots = hall.shape[2]
    members = groups * local
    halo = STEPS
    m = lax.axis_index("mem")
    r = lax.axis_index("reg")
    up = lax.rem(r + regions - 1, regions)
    down = lax.rem(r + 1, regions)

    barrier = pltpu.get_barrier_semaphore()
    for side in (up, down):
        pl.semaphore_signal(barrier, inc=1, device_id=(m, side), device_id_type=MESH)
    for j in range(1, groups):
        pl.semaphore_signal(barrier, inc=1, device_id=(lax.rem(m + j, groups), r), device_id_type=MESH)
    own_load = pltpu.make_async_copy(mem_ref, padded.at[pl.ds(halo, lines)], local_sem.at[0])
    own_load.start()
    cells_out[...] = jnp.broadcast_to(cell_ref[0], cells_out.shape)
    slot = lax.broadcasted_iota(jnp.int32, (1, slots), 1)
    own_prec = jnp.where(slot < cnt_ref[...], rinv_ref[0], 0.0)
    reach = (loc_ref[0].astype(F32) + 1.0) * 0.25
    far_prec = (own_prec * jnp.exp(-(reach * reach))).astype(BF16).astype(F32)
    own_val = val_ref[0].astype(F32)
    info_row = lax.broadcasted_iota(jnp.int32, info_out.shape, 0)
    info_out[...] = jnp.where(info_row == 0, own_val, far_prec)
    pl.semaphore_wait(barrier, groups + 1)

    copies = []

    def send(src, dst, target):
        at = len(copies)
        copy = pltpu.make_async_remote_copy(
            src_ref=src, dst_ref=dst, send_sem=send_sem.at[at], recv_sem=recv_sem.at[at],
            device_id=target, device_id_type=MESH,
        )
        copy.start()
        copies.append(copy)
        return copy

    above, below = (m, up), (m, down)
    halo_top = send(mem_ref.at[pl.ds(lines - halo, halo)], padded.at[pl.ds(0, halo)], below)
    halo_bottom = send(mem_ref.at[pl.ds(0, halo)], padded.at[pl.ds(lines + halo, halo)], above)
    coef_top = [
        send(ref.at[pl.ds(lines - 8, 8)], coef_in.at[0, i], below)
        for i, ref in enumerate((dif_ref, adv_ref))
    ]
    coef_bottom = [
        send(ref.at[pl.ds(0, 8)], coef_in.at[1, i], above)
        for i, ref in enumerate((dif_ref, adv_ref))
    ]
    cell_copies = [
        send(cells_out, cells_in.at[j - 1], (lax.rem(m + j, groups), r)) for j in range(1, groups)
    ]
    info_copies = [
        send(info_out, info_in.at[0], below),
        send(info_out, info_in.at[1], above),
    ]

    def put_coef(base, d, a):
        rows = pl.ds(base, d.shape[0])
        coef[0, rows] = 1.0 - 4.0 * d
        coef[1, rows] = d + 0.5 * a
        coef[2, rows] = d - 0.5 * a
        coef[3, rows] = d

    put_coef(8, dif_ref[...], adv_ref[...])

    def step(src, dst, shift, low, high):
        def body(p, _):
            k = [coef[i, pl.ds(p + 8 - halo, 1), :] for i in range(4)]
            for at in range(0, local, MEMBER_BLOCK):
                block = pl.ds(at, MEMBER_BLOCK)
                c = src[p, block, :].astype(F32)
                n = src[p - 1, block, :].astype(F32)
                s = src[p + 1, block, :].astype(F32)
                sides = pltpu.roll(c, width - 1, 1) + pltpu.roll(c, 1, 1)
                value = k[0] * c + k[1] * n + k[2] * s + k[3] * sides
                dst[p - shift, block, :] = value.astype(dst.dtype)
            return 0

        lax.fori_loop(low, high, body, 0)

    own_load.wait()

    def early_at(g):
        return halo * (1 - (g + groups - 1) // groups)

    def late_at(g):
        return (patch - halo) * ((g + groups - 1) // groups)

    early = patch - halo

    def interior(g):
        low = g * patch + early_at(g) + halo
        high = low + early
        step(padded, first, 0, low - 2, high + 2)
        step(first, second, 0, low - 1, high + 1)
        step(second, fc, halo, low, high)

    def edge(g):
        inner = (g + groups - 1) // groups
        end = g * patch + patch
        for s, (src, dst, shift) in enumerate(((padded, first, 0), (first, second, 0), (second, fc, halo))):
            low = (s - 2) * (1 - inner) + (end - 1 - s) * inner + halo
            step(src, dst, shift, low, low + halo)

    forwards = []

    def forward(j, late, at, count):
        g = lax.rem(m + j, groups)
        at = at + (late_at(g) if late else early_at(g))
        forwards.append((late, send(
            fc.at[pl.ds(g * patch + at, count)],
            states.at[pl.ds(at, count), pl.ds(m * local, local)],
            (g, r),
        )))

    for j in range(1, groups):
        interior(lax.rem(m + j, groups))
        forward(j, False, 0, early - 2)

    halo_top.wait_recv()
    halo_bottom.wait_recv()
    for copy in coef_top + coef_bottom:
        copy.wait_recv()
    put_coef(0, coef_in[0, 0], coef_in[0, 1])
    put_coef(lines + 8, coef_in[1, 0], coef_in[1, 1])

    cell_index = lax.broadcasted_iota(jnp.int32, (patch * width, slots), 0)

    def observe(g, cells):
        flat = jnp.concatenate([fc[g * patch + l] for l in range(patch)], axis=1)
        pick = jnp.where(cell_index == cells, 1.0, 0.0).astype(BF16)
        return jnp.dot(flat, pick, preferred_element_type=F32).astype(BF16)

    hx = []
    for j in range(1, groups):
        g = lax.rem(m + j, groups)
        edge(g)
        cell_copies[groups - j - 1].wait_recv()
        hsend[j - 1] = observe(g, cells_in[groups - j - 1, 0:1, :])
        hx.append(send(hsend.at[j - 1], hall.at[0, pl.ds(m * local, local)], (g, r)))
        forward(j, False, early - 2, 1)
    own_rows = pl.ds(pl.multiple_of(m * local, local), local)
    interior(m)
    edge(m)
    hall[0, own_rows, :] = observe(m, cell_ref[0])

    def relay(block):
        rows = pl.ds(block * local, local)
        return [
            send(hall.at[0, rows], hall.at[1, rows], below),
            send(hall.at[0, rows], hall.at[2, rows], above),
        ]

    relays = relay(m)
    for l in range(patch):
        states[l, own_rows, :] = fc[m * patch + l]
    for j in range(1, groups):
        hx[j - 1].wait_recv()
        relays += relay(lax.rem(m + groups - j, groups))
        forward(j, False, early - 1, 1)
        forward(j, True, 0, halo)

    row_id = lax.broadcasted_iota(jnp.int32, (members, members), 0)
    col_id = lax.broadcasted_iota(jnp.int32, (members, members), 1)
    eye = jnp.where(row_id == col_id, 1.0, 0.0)

    def gram(h, value, prec):
        h = h.astype(F32)
        hbar = jnp.sum(h, axis=0, keepdims=True) * (1.0 / members)
        y = h - hbar
        weighted = y * prec
        part = lax.dot_general(
            weighted.astype(BF16), y.astype(BF16), (((1,), (1,)), ((), ())),
            preferred_element_type=F32,
        )
        return part, jnp.sum(weighted * (value - hbar), axis=1, keepdims=True)

    system, force = gram(hall[0], own_val, own_prec)
    system = system + (members - 1.0) * eye

    def perturb(low, count):
        for i in range(count):
            lane = pl.ds(pl.multiple_of((low + i) * width, width), width)
            x = states[low + i].astype(F32)
            mean = jnp.sum(x, axis=0, keepdims=True) * (1.0 / members)
            xbar[0:1, lane] = mean
            xb[:, lane] = (x - mean).astype(BF16)

    for late, copy in forwards[:2 * (groups - 1)]:
        copy.wait_recv()
    perturb(early_at(m), early - 1)
    for copy in info_copies + relays:
        copy.wait_recv()
    for side in range(2):
        part, more = gram(hall[1 + side], info_in[side, 0:1, :], info_in[side, 1:2, :])
        system, force = system + part, force + more
    total = jnp.sum(jnp.sum(system * system, axis=0, keepdims=True), axis=1, keepdims=True)
    inv_scale = lax.rsqrt(total)
    y1 = system * inv_scale
    y1b = y1.astype(BF16)
    y2 = jnp.dot(y1b, y1b, preferred_element_type=F32)
    tail = (0.0625 * y2 - 0.5625 * y1).astype(BF16)
    z = 2.25 * eye - 2.4375 * y1 + 1.6875 * y2 + jnp.dot(
        y2.astype(BF16), tail, preferred_element_type=F32
    )
    half = jnp.sum(z * force, axis=0, keepdims=True)
    mean_col = jnp.sum(z * half, axis=1, keepdims=True) * inv_scale
    mean_row = jnp.sum(eye * mean_col, axis=0, keepdims=True)
    wt[...] = (jnp.sqrt((members - 1.0) * inv_scale) * z + mean_row).astype(BF16)

    def result(g, l, count):
        lane = pl.ds(pl.multiple_of(l * width, width), count * width)
        rows = pl.ds(pl.multiple_of(g * local, local), local)
        return xbar[0:1, lane] + jnp.dot(wt[rows, :], xb[:, lane], preferred_element_type=F32)

    cuts = ((False, 0, early - 3), (False, early - 3, 2), (False, early - 1, 1), (True, 0, halo))

    def row_of(g, cut):
        return cut[1] + (late_at(g) if cut[0] else early_at(g))

    returns = []
    for cut in cuts:
        l, count = row_of(m, cut), cut[2]
        if cut[0]:
            for late, copy in forwards[2 * (groups - 1):]:
                if late:
                    copy.wait_recv()
            perturb(late_at(m), halo)
        elif cut[1] == early - 1:
            for late, copy in forwards[2 * (groups - 1):]:
                if not late:
                    copy.wait_recv()
            perturb(l, 1)
        for j in range(1, groups):
            g = lax.rem(m + j, groups)
            value = result(g, l, count).astype(BF16)
            for i in range(count):
                ret_out[j - 1, l + i] = value[:, i * width:(i + 1) * width]
            rows = pl.ds(l, count)
            returns.append((j, cut, send(ret_out.at[j - 1, rows], ret_in.at[j - 1, rows], (g, r))))
    for cut in cuts:
        l, count = row_of(m, cut), cut[2]
        value = result(m, l, count)
        for i in range(count):
            out_ref[m * patch + l + i] = value[:, i * width:(i + 1) * width]
    for j, cut, copy in returns:
        copy.wait_recv()
        g = lax.rem(m + groups - j, groups)
        l = row_of(g, cut)
        for i in range(cut[2]):
            out_ref[g * patch + l + i] = ret_in[j - 1, l + i].astype(F32)
    for copy in copies:
        copy.wait_send()


def on_device(groups, regions, members, diffusivity, advection, obs_value, obs_rinv, obs_cell, obs_count, loc_index):
    local, lines, width = members.shape
    slots = obs_cell.shape[-1]
    patch = lines // groups
    total = groups * local
    partners = groups - 1
    count = 8 + partners + 4 * partners + partners + 2 * groups + 4 * partners
    vmem = pl.BlockSpec(memory_space=pltpu.VMEM)
    flops = 2 * total * total * (3 * slots + 2 * total + patch * width)
    result = pl.pallas_call(
        functools.partial(kernel, groups, regions),
        out_shape=jax.ShapeDtypeStruct((lines, local, width), F32),
        in_specs=[pl.BlockSpec(memory_space=pl.ANY)] + [vmem] * 7,
        out_specs=vmem,
        scratch_shapes=[
            pltpu.VMEM((lines + 2 * STEPS, local, width), BF16),
            pltpu.VMEM((lines + 2 * STEPS, local, width), F32),
            pltpu.VMEM((lines + 2 * STEPS, local, width), F32),
            pltpu.VMEM((lines, local, width), BF16),
            pltpu.VMEM((patch, total, width), BF16),
            pltpu.VMEM((4, lines + 16, width), F32),
            pltpu.VMEM((2, 2, 8, width), F32),
            pltpu.VMEM((8, slots), jnp.int32),
            pltpu.VMEM((partners, 8, slots), jnp.int32),
            pltpu.VMEM((8, slots), F32),
            pltpu.VMEM((2, 8, slots), F32),
            pltpu.VMEM((partners, local, slots), BF16),
            pltpu.VMEM((3, total, slots), BF16),
            pltpu.VMEM((total, total), BF16),
            pltpu.VMEM((total, patch * width), BF16),
            pltpu.VMEM((8, patch * width), F32),
            pltpu.VMEM((partners, patch, local, width), BF16),
            pltpu.VMEM((partners, patch, local, width), BF16),
            pltpu.SemaphoreType.DMA((1,)),
            pltpu.SemaphoreType.DMA((count,)),
            pltpu.SemaphoreType.DMA((count,)),
        ],
        compiler_params=pltpu.CompilerParams(
            collective_id=0, has_side_effects=True, vmem_limit_bytes=48 * 1024 * 1024
        ),
        cost_estimate=pl.CostEstimate(flops=flops, bytes_accessed=6 * lines * local * width, transcendentals=0),
    )(
        jnp.transpose(members, (1, 0, 2)), diffusivity, advection, obs_value, obs_rinv,
        obs_cell, obs_count, loc_index,
    )
    return jnp.transpose(result, (1, 0, 2))


def solution(mesh):
    return jax.shard_map(
        functools.partial(on_device, mesh.shape["mem"], mesh.shape["reg"]),
        mesh=mesh,
        in_specs=(
            P("mem", "reg", None),
            P("reg", None),
            P("reg", None),
            P("reg", "mem", None),
            P("reg", "mem", None),
            P("reg", "mem", None),
            P("reg", "mem"),
            P("reg", "mem", None),
        ),
        out_specs=P("mem", "reg", None),
        check_vma=False,
    )
```

```python
import functools

import jax
import jax.numpy as jnp
from jax import lax
from jax.experimental import pallas as pl
from jax.experimental.pallas import tpu as pltpu
from jax.sharding import PartitionSpec as P

STEPS = 3
MESH = pl.DeviceIdType.MESH
F32 = jnp.float32
BF16 = jnp.bfloat16
MEMBER_BLOCK = 64


def kernel(
    groups, regions,
    mem_ref, dif_ref, adv_ref, val_ref, rinv_ref, cell_ref, cnt_ref, loc_ref,
    out_ref,
    padded, first, second, fc, states, coef, coef_in, cells_out, cells_in,
    info_out, info_in, hsend, hall, wt, xb, xbar, ret_out, ret_in,
    local_sem, send_sem, recv_sem,
):
    lines, local, width = mem_ref.shape
    patch = lines // groups
    slots = hall.shape[2]
    members = groups * local
    halo = STEPS
    m = lax.axis_index("mem")
    r = lax.axis_index("reg")
    up = lax.rem(r + regions - 1, regions)
    down = lax.rem(r + 1, regions)

    barrier = pltpu.get_barrier_semaphore()
    for side in (up, down):
        pl.semaphore_signal(barrier, inc=1, device_id=(m, side), device_id_type=MESH)
    for j in range(1, groups):
        pl.semaphore_signal(barrier, inc=1, device_id=(lax.rem(m + j, groups), r), device_id_type=MESH)
    own_load = pltpu.make_async_copy(mem_ref, padded.at[pl.ds(halo, lines)], local_sem.at[0])
    own_load.start()
    cells_out[...] = jnp.broadcast_to(cell_ref[0], cells_out.shape)
    slot = lax.broadcasted_iota(jnp.int32, (1, slots), 1)
    own_prec = jnp.where(slot < cnt_ref[...], rinv_ref[0], 0.0)
    reach = (loc_ref[0].astype(F32) + 1.0) * 0.25
    far_prec = (own_prec * jnp.exp(-(reach * reach))).astype(BF16).astype(F32)
    own_val = val_ref[0].astype(F32)
    info_row = lax.broadcasted_iota(jnp.int32, info_out.shape, 0)
    info_out[...] = jnp.where(info_row == 0, own_val, far_prec)
    def put_coef(base, d, a):
        rows = pl.ds(base, d.shape[0])
        coef[0, rows] = 1.0 - 4.0 * d
        coef[1, rows] = d + 0.5 * a
        coef[2, rows] = d - 0.5 * a
        coef[3, rows] = d

    put_coef(8, dif_ref[...], adv_ref[...])

    def step(src, dst, shift, low, high):
        def body(p, _):
            k = [coef[i, pl.ds(p + 8 - halo, 1), :] for i in range(4)]
            for at in range(0, local, MEMBER_BLOCK):
                block = pl.ds(at, MEMBER_BLOCK)
                c = src[p, block, :].astype(F32)
                n = src[p - 1, block, :].astype(F32)
                s = src[p + 1, block, :].astype(F32)
                sides = pltpu.roll(c, width - 1, 1) + pltpu.roll(c, 1, 1)
                value = k[0] * c + k[1] * n + k[2] * s + k[3] * sides
                dst[p - shift, block, :] = value.astype(dst.dtype)
            return 0

        lax.fori_loop(low, high, body, 0)

    own_load.wait()

    def early_at(g):
        return halo * (1 - (g + groups - 1) // groups)

    def late_at(g):
        return (patch - halo) * ((g + groups - 1) // groups)

    early = patch - halo

    def interior(g):
        low = g * patch + early_at(g) + halo
        high = low + early
        step(padded, first, 0, low - 2, high + 2)
        step(first, second, 0, low - 1, high + 1)
        step(second, fc, halo, low, high)

    def edge(g):
        inner = (g + groups - 1) // groups
        end = g * patch + patch
        for s, (src, dst, shift) in enumerate(((padded, first, 0), (first, second, 0), (second, fc, halo))):
            low = (s - 2) * (1 - inner) + (end - 1 - s) * inner + halo
            step(src, dst, shift, low, low + halo)

    for j in range(1, groups):
        interior(lax.rem(m + j, groups))

    pl.semaphore_wait(barrier, groups + 1)

    copies = []

    def send(src, dst, target):
        at = len(copies)
        copy = pltpu.make_async_remote_copy(
            src_ref=src, dst_ref=dst, send_sem=send_sem.at[at], recv_sem=recv_sem.at[at],
            device_id=target, device_id_type=MESH,
        )
        copy.start()
        copies.append(copy)
        return copy

    above, below = (m, up), (m, down)
    halo_top = send(mem_ref.at[pl.ds(lines - halo, halo)], padded.at[pl.ds(0, halo)], below)
    halo_bottom = send(mem_ref.at[pl.ds(0, halo)], padded.at[pl.ds(lines + halo, halo)], above)
    coef_top = [
        send(ref.at[pl.ds(lines - 8, 8)], coef_in.at[0, i], below)
        for i, ref in enumerate((dif_ref, adv_ref))
    ]
    coef_bottom = [
        send(ref.at[pl.ds(0, 8)], coef_in.at[1, i], above)
        for i, ref in enumerate((dif_ref, adv_ref))
    ]
    cell_copies = [
        send(cells_out, cells_in.at[j - 1], (lax.rem(m + j, groups), r)) for j in range(1, groups)
    ]
    info_copies = [
        send(info_out, info_in.at[0], below),
        send(info_out, info_in.at[1], above),
    ]

    forwards = []

    def forward(j, late, at, count):
        g = lax.rem(m + j, groups)
        at = at + (late_at(g) if late else early_at(g))
        forwards.append((late, send(
            fc.at[pl.ds(g * patch + at, count)],
            states.at[pl.ds(at, count), pl.ds(m * local, local)],
            (g, r),
        )))

    for j in range(1, groups):
        forward(j, False, 0, early - 1)
    interior(m)

    halo_top.wait_recv()
    halo_bottom.wait_recv()
    for copy in coef_top + coef_bottom:
        copy.wait_recv()
    put_coef(0, coef_in[0, 0], coef_in[0, 1])
    put_coef(lines + 8, coef_in[1, 0], coef_in[1, 1])

    cell_index = lax.broadcasted_iota(jnp.int32, (patch * width, slots), 0)

    def observe(g, cells):
        flat = jnp.concatenate([fc[g * patch + l] for l in range(patch)], axis=1)
        pick = jnp.where(cell_index == cells, 1.0, 0.0).astype(BF16)
        return jnp.dot(flat, pick, preferred_element_type=F32).astype(BF16)

    hx = []
    for j in range(1, groups):
        g = lax.rem(m + j, groups)
        edge(g)
        cell_copies[groups - j - 1].wait_recv()
        hsend[j - 1] = observe(g, cells_in[groups - j - 1, 0:1, :])
        hx.append(send(hsend.at[j - 1], hall.at[0, pl.ds(m * local, local)], (g, r)))
        forward(j, False, early - 1, 1)
    own_rows = pl.ds(pl.multiple_of(m * local, local), local)
    edge(m)
    hall[0, own_rows, :] = observe(m, cell_ref[0])

    def relay(block):
        rows = pl.ds(block * local, local)
        return [
            send(hall.at[0, rows], hall.at[1, rows], below),
            send(hall.at[0, rows], hall.at[2, rows], above),
        ]

    relays = relay(m)
    for l in range(patch):
        states[l, own_rows, :] = fc[m * patch + l]
    for j in range(1, groups):
        hx[j - 1].wait_recv()
        relays += relay(lax.rem(m + groups - j, groups))
        forward(j, True, 0, halo)

    row_id = lax.broadcasted_iota(jnp.int32, (members, members), 0)
    col_id = lax.broadcasted_iota(jnp.int32, (members, members), 1)
    eye = jnp.where(row_id == col_id, 1.0, 0.0)

    def gram(h, value, prec):
        h = h.astype(F32)
        hbar = jnp.sum(h, axis=0, keepdims=True) * (1.0 / members)
        y = h - hbar
        weighted = y * prec
        part = lax.dot_general(
            weighted.astype(BF16), y.astype(BF16), (((1,), (1,)), ((), ())),
            preferred_element_type=F32,
        )
        return part, jnp.sum(weighted * (value - hbar), axis=1, keepdims=True)

    system, force = gram(hall[0], own_val, own_prec)
    system = system + (members - 1.0) * eye

    def perturb(low, count):
        for i in range(count):
            lane = pl.ds(pl.multiple_of((low + i) * width, width), width)
            x = states[low + i].astype(F32)
            mean = jnp.sum(x, axis=0, keepdims=True) * (1.0 / members)
            xbar[0:1, lane] = mean
            xb[:, lane] = (x - mean).astype(BF16)

    for late, copy in forwards[:groups - 1]:
        copy.wait_recv()
    perturb(early_at(m), early - 1)
    for copy in info_copies + relays:
        copy.wait_recv()
    for side in range(2):
        part, more = gram(hall[1 + side], info_in[side, 0:1, :], info_in[side, 1:2, :])
        system, force = system + part, force + more
    total = jnp.sum(jnp.sum(system * system, axis=0, keepdims=True), axis=1, keepdims=True)
    inv_scale = lax.rsqrt(total)
    y1 = system * inv_scale
    y1b = y1.astype(BF16)
    y2 = jnp.dot(y1b, y1b, preferred_element_type=F32)
    tail = (0.0625 * y2 - 0.5625 * y1).astype(BF16)
    z = 2.25 * eye - 2.4375 * y1 + 1.6875 * y2 + jnp.dot(
        y2.astype(BF16), tail, preferred_element_type=F32
    )
    half = jnp.sum(z * force, axis=0, keepdims=True)
    mean_col = jnp.sum(z * half, axis=1, keepdims=True) * inv_scale
    mean_row = jnp.sum(eye * mean_col, axis=0, keepdims=True)
    wt[...] = (jnp.sqrt((members - 1.0) * inv_scale) * z + mean_row).astype(BF16)

    def result(g, l, count):
        lane = pl.ds(pl.multiple_of(l * width, width), count * width)
        rows = pl.ds(pl.multiple_of(g * local, local), local)
        return xbar[0:1, lane] + jnp.dot(wt[rows, :], xb[:, lane], preferred_element_type=F32)

    cuts = ((False, 0, early - 3), (False, early - 3, 2), (False, early - 1, 1), (True, 0, halo))

    def row_of(g, cut):
        return cut[1] + (late_at(g) if cut[0] else early_at(g))

    def place(line, value):
        out_ref[pl.ds(line, local, stride=lines), :] = value

    returns = []
    for cut in cuts:
        l, count = row_of(m, cut), cut[2]
        if cut[0]:
            for late, copy in forwards[groups - 1:]:
                if late:
                    copy.wait_recv()
            perturb(late_at(m), halo)
        elif cut[1] == early - 1:
            for late, copy in forwards[groups - 1:]:
                if not late:
                    copy.wait_recv()
            perturb(l, 1)
        for j in range(1, groups):
            g = lax.rem(m + j, groups)
            value = result(g, l, count).astype(BF16)
            for i in range(count):
                ret_out[j - 1, l + i] = value[:, i * width:(i + 1) * width]
            rows = pl.ds(l, count)
            returns.append((j, cut, send(ret_out.at[j - 1, rows], ret_in.at[j - 1, rows], (g, r))))
    for cut in cuts:
        l, count = row_of(m, cut), cut[2]
        value = result(m, l, count)
        for i in range(count):
            place(m * patch + l + i, value[:, i * width:(i + 1) * width])
    for j, cut, copy in returns:
        copy.wait_recv()
        g = lax.rem(m + groups - j, groups)
        l = row_of(g, cut)
        for i in range(cut[2]):
            place(g * patch + l + i, ret_in[j - 1, l + i].astype(F32))
    for copy in copies:
        copy.wait_send()


def on_device(groups, regions, members, diffusivity, advection, obs_value, obs_rinv, obs_cell, obs_count, loc_index):
    local, lines, width = members.shape
    slots = obs_cell.shape[-1]
    patch = lines // groups
    total = groups * local
    partners = groups - 1
    count = 8 + partners + 3 * partners + partners + 2 * groups + 4 * partners
    vmem = pl.BlockSpec(memory_space=pltpu.VMEM)
    flops = 2 * total * total * (3 * slots + 2 * total + patch * width)
    result = pl.pallas_call(
        functools.partial(kernel, groups, regions),
        out_shape=jax.ShapeDtypeStruct((local * lines, width), F32),
        in_specs=[pl.BlockSpec(memory_space=pl.ANY)] + [vmem] * 7,
        out_specs=vmem,
        scratch_shapes=[
            pltpu.VMEM((lines + 2 * STEPS, local, width), BF16),
            pltpu.VMEM((lines + 2 * STEPS, local, width), F32),
            pltpu.VMEM((lines + 2 * STEPS, local, width), F32),
            pltpu.VMEM((lines, local, width), BF16),
            pltpu.VMEM((patch, total, width), BF16),
            pltpu.VMEM((4, lines + 16, width), F32),
            pltpu.VMEM((2, 2, 8, width), F32),
            pltpu.VMEM((8, slots), jnp.int32),
            pltpu.VMEM((partners, 8, slots), jnp.int32),
            pltpu.VMEM((8, slots), F32),
            pltpu.VMEM((2, 8, slots), F32),
            pltpu.VMEM((partners, local, slots), BF16),
            pltpu.VMEM((3, total, slots), BF16),
            pltpu.VMEM((total, total), BF16),
            pltpu.VMEM((total, patch * width), BF16),
            pltpu.VMEM((8, patch * width), F32),
            pltpu.VMEM((partners, patch, local, width), BF16),
            pltpu.VMEM((partners, patch, local, width), BF16),
            pltpu.SemaphoreType.DMA((1,)),
            pltpu.SemaphoreType.DMA((count,)),
            pltpu.SemaphoreType.DMA((count,)),
        ],
        compiler_params=pltpu.CompilerParams(
            collective_id=0, has_side_effects=True, vmem_limit_bytes=48 * 1024 * 1024
        ),
        cost_estimate=pl.CostEstimate(flops=flops, bytes_accessed=6 * lines * local * width, transcendentals=0),
    )(
        jnp.transpose(members, (1, 0, 2)), diffusivity, advection, obs_value, obs_rinv,
        obs_cell, obs_count, loc_index,
    )
    return result.reshape(local, lines, width)


def solution(mesh):
    return jax.shard_map(
        functools.partial(on_device, mesh.shape["mem"], mesh.shape["reg"]),
        mesh=mesh,
        in_specs=(
            P("mem", "reg", None),
            P("reg", None),
            P("reg", None),
            P("reg", "mem", None),
            P("reg", "mem", None),
            P("reg", "mem", None),
            P("reg", "mem"),
            P("reg", "mem", None),
        ),
        out_specs=P("mem", "reg", None),
        check_vma=False,
    )
```

```python
import functools

import jax
import jax.numpy as jnp
from jax import lax
from jax.experimental import pallas as pl
from jax.experimental.pallas import tpu as pltpu
from jax.sharding import PartitionSpec as P

STEPS = 3
MESH = pl.DeviceIdType.MESH
F32 = jnp.float32
BF16 = jnp.bfloat16
MEMBER_BLOCK = 64


def kernel(
    groups, regions,
    mem_ref, dif_ref, adv_ref, val_ref, rinv_ref, cell_ref, cnt_ref, loc_ref,
    out_ref,
    padded, first, second, fc, states, coef, coef_in, cells_out, cells_in,
    info_out, info_in, hsend, hall, wt, xb, xbar, ret_out, ret_in,
    local_sem, send_sem, recv_sem,
):
    lines, local, width = mem_ref.shape
    patch = lines // groups
    slots = hall.shape[2]
    members = groups * local
    halo = STEPS
    m = lax.axis_index("mem")
    r = lax.axis_index("reg")
    up = lax.rem(r + regions - 1, regions)
    down = lax.rem(r + 1, regions)

    barrier = pltpu.get_barrier_semaphore()
    for side in (up, down):
        pl.semaphore_signal(barrier, inc=1, device_id=(m, side), device_id_type=MESH)
    for j in range(1, groups):
        pl.semaphore_signal(barrier, inc=1, device_id=(lax.rem(m + j, groups), r), device_id_type=MESH)
    own_load = pltpu.make_async_copy(mem_ref, padded.at[pl.ds(halo, lines)], local_sem.at[0])
    own_load.start()
    cells_out[...] = jnp.broadcast_to(cell_ref[0], cells_out.shape)
    slot = lax.broadcasted_iota(jnp.int32, (1, slots), 1)
    own_prec = jnp.where(slot < cnt_ref[...], rinv_ref[0], 0.0)
    reach = (loc_ref[0].astype(F32) + 1.0) * 0.25
    far_prec = (own_prec * jnp.exp(-(reach * reach))).astype(BF16).astype(F32)
    own_val = val_ref[0].astype(F32)
    info_row = lax.broadcasted_iota(jnp.int32, info_out.shape, 0)
    info_out[...] = jnp.where(info_row == 0, own_val, far_prec)
    def put_coef(base, d, a):
        rows = pl.ds(base, d.shape[0])
        coef[0, rows] = 1.0 - 4.0 * d
        coef[1, rows] = d + 0.5 * a
        coef[2, rows] = d - 0.5 * a
        coef[3, rows] = d

    put_coef(8, dif_ref[...], adv_ref[...])

    def step(src, dst, shift, low, high):
        def body(p, _):
            k = [coef[i, pl.ds(p + 8 - halo, 1), :] for i in range(4)]
            for at in range(0, local, MEMBER_BLOCK):
                block = pl.ds(at, MEMBER_BLOCK)
                c = src[p, block, :].astype(F32)
                n = src[p - 1, block, :].astype(F32)
                s = src[p + 1, block, :].astype(F32)
                sides = pltpu.roll(c, width - 1, 1) + pltpu.roll(c, 1, 1)
                value = k[0] * c + k[1] * n + k[2] * s + k[3] * sides
                dst[p - shift, block, :] = value.astype(dst.dtype)
            return 0

        lax.fori_loop(low, high, body, 0)

    own_load.wait()

    def early_at(g):
        return halo * (1 - (g + groups - 1) // groups)

    def late_at(g):
        return (patch - halo) * ((g + groups - 1) // groups)

    early = patch - halo

    def interior(g):
        low = g * patch + early_at(g) + halo
        high = low + early
        step(padded, first, 0, low - 2, high + 2)
        step(first, second, 0, low - 1, high + 1)
        step(second, fc, halo, low, high)

    def edge(g):
        inner = (g + groups - 1) // groups
        end = g * patch + patch
        for s, (src, dst, shift) in enumerate(((padded, first, 0), (first, second, 0), (second, fc, halo))):
            low = (s - 2) * (1 - inner) + (end - 1 - s) * inner + halo
            step(src, dst, shift, low, low + halo)

    for j in range(1, groups):
        interior(lax.rem(m + j, groups))

    pl.semaphore_wait(barrier, groups + 1)

    copies = []

    def send(src, dst, target):
        at = len(copies)
        copy = pltpu.make_async_remote_copy(
            src_ref=src, dst_ref=dst, send_sem=send_sem.at[at], recv_sem=recv_sem.at[at],
            device_id=target, device_id_type=MESH,
        )
        copy.start()
        copies.append(copy)
        return copy

    above, below = (m, up), (m, down)
    halo_top = send(mem_ref.at[pl.ds(lines - halo, halo)], padded.at[pl.ds(0, halo)], below)
    halo_bottom = send(mem_ref.at[pl.ds(0, halo)], padded.at[pl.ds(lines + halo, halo)], above)
    coef_top = [
        send(ref.at[pl.ds(lines - 8, 8)], coef_in.at[0, i], below)
        for i, ref in enumerate((dif_ref, adv_ref))
    ]
    coef_bottom = [
        send(ref.at[pl.ds(0, 8)], coef_in.at[1, i], above)
        for i, ref in enumerate((dif_ref, adv_ref))
    ]
    cell_copies = [
        send(cells_out, cells_in.at[j - 1], (lax.rem(m + j, groups), r)) for j in range(1, groups)
    ]
    info_copies = [
        send(info_out, info_in.at[0], below),
        send(info_out, info_in.at[1], above),
    ]

    forwards = []

    def forward(j, late, at, count):
        g = lax.rem(m + j, groups)
        at = at + (late_at(g) if late else early_at(g))
        forwards.append((late, send(
            fc.at[pl.ds(g * patch + at, count)],
            states.at[pl.ds(at, count), pl.ds(m * local, local)],
            (g, r),
        )))

    for j in range(1, groups):
        forward(j, False, 0, early - 2)
    interior(m)

    halo_top.wait_recv()
    halo_bottom.wait_recv()
    for copy in coef_top + coef_bottom:
        copy.wait_recv()
    put_coef(0, coef_in[0, 0], coef_in[0, 1])
    put_coef(lines + 8, coef_in[1, 0], coef_in[1, 1])

    cell_index = lax.broadcasted_iota(jnp.int32, (patch * width, slots), 0)

    def observe(g, cells):
        flat = jnp.concatenate([fc[g * patch + l] for l in range(patch)], axis=1)
        pick = jnp.where(cell_index == cells, 1.0, 0.0).astype(BF16)
        return jnp.dot(flat, pick, preferred_element_type=F32).astype(BF16)

    half_rows = local // 2
    hx = []
    for j in range(1, groups):
        g = lax.rem(m + j, groups)
        edge(g)
        cell_copies[groups - j - 1].wait_recv()
        hsend[j - 1] = observe(g, cells_in[groups - j - 1, 0:1, :])
        for at in range(0, local, half_rows):
            hx.append((j, at, send(
                hsend.at[j - 1, pl.ds(at, half_rows)], hall.at[0, pl.ds(m * local + at, half_rows)], (g, r)
            )))
        forward(j, False, early - 2, 2)
    own_rows = pl.ds(pl.multiple_of(m * local, local), local)
    edge(m)
    hall[0, own_rows, :] = observe(m, cell_ref[0])

    def relay(start, count):
        rows = pl.ds(start, count)
        return [
            send(hall.at[0, rows], hall.at[1, rows], below),
            send(hall.at[0, rows], hall.at[2, rows], above),
        ]

    relays = relay(m * local, local)
    for l in range(patch):
        states[l, own_rows, :] = fc[m * patch + l]
    for j, at, copy in hx:
        copy.wait_recv()
        relays += relay(lax.rem(m + groups - j, groups) * local + at, half_rows)
    for j in range(1, groups):
        forward(j, True, 0, halo)

    row_id = lax.broadcasted_iota(jnp.int32, (members, members), 0)
    col_id = lax.broadcasted_iota(jnp.int32, (members, members), 1)
    eye = jnp.where(row_id == col_id, 1.0, 0.0)

    def gram(h, value, prec):
        h = h.astype(F32)
        hbar = jnp.sum(h, axis=0, keepdims=True) * (1.0 / members)
        y = h - hbar
        weighted = y * prec
        part = lax.dot_general(
            weighted.astype(BF16), y.astype(BF16), (((1,), (1,)), ((), ())),
            preferred_element_type=F32,
        )
        return part, jnp.sum(weighted * (value - hbar), axis=1, keepdims=True)

    system, force = gram(hall[0], own_val, own_prec)
    system = system + (members - 1.0) * eye

    def perturb(low, count):
        for i in range(count):
            lane = pl.ds(pl.multiple_of((low + i) * width, width), width)
            x = states[low + i].astype(F32)
            mean = jnp.sum(x, axis=0, keepdims=True) * (1.0 / members)
            xbar[0:1, lane] = mean
            xb[:, lane] = (x - mean).astype(BF16)

    for late, copy in forwards[:groups - 1]:
        copy.wait_recv()
    perturb(early_at(m), early - 2)
    for side in range(2):
        for copy in [info_copies[side]] + relays[side::2]:
            copy.wait_recv()
        part, more = gram(hall[1 + side], info_in[side, 0:1, :], info_in[side, 1:2, :])
        system, force = system + part, force + more
    total = jnp.sum(jnp.sum(system * system, axis=0, keepdims=True), axis=1, keepdims=True)
    inv_scale = lax.rsqrt(total)
    y1 = system * inv_scale
    y1b = y1.astype(BF16)
    y2 = jnp.dot(y1b, y1b, preferred_element_type=F32)
    tail = (0.0625 * y2 - 0.5625 * y1).astype(BF16)
    z = 2.25 * eye - 2.4375 * y1 + 1.6875 * y2 + jnp.dot(
        y2.astype(BF16), tail, preferred_element_type=F32
    )
    half = jnp.sum(z * force, axis=0, keepdims=True)
    mean_col = jnp.sum(z * half, axis=1, keepdims=True) * inv_scale
    mean_row = jnp.sum(eye * mean_col, axis=0, keepdims=True)
    wt[...] = (jnp.sqrt((members - 1.0) * inv_scale) * z + mean_row).astype(BF16)

    def result(g, l, count):
        lane = pl.ds(pl.multiple_of(l * width, width), count * width)
        rows = pl.ds(pl.multiple_of(g * local, local), local)
        return xbar[0:1, lane] + jnp.dot(wt[rows, :], xb[:, lane], preferred_element_type=F32)

    cuts = ((False, 0, early - 2), (False, early - 2, 2), (True, 0, halo - 1), (True, halo - 1, 1))

    def row_of(g, cut):
        return cut[1] + (late_at(g) if cut[0] else early_at(g))

    def place(line, value):
        out_ref[pl.ds(line, local, stride=lines), :] = value

    returns = []
    for cut in cuts:
        l, count = row_of(m, cut), cut[2]
        if cut == cuts[1]:
            for late, copy in forwards[groups - 1:]:
                if not late:
                    copy.wait_recv()
            perturb(l, count)
        elif cut == cuts[2]:
            for late, copy in forwards[groups - 1:]:
                if late:
                    copy.wait_recv()
            perturb(late_at(m), halo)
        for j in range(1, groups):
            g = lax.rem(m + j, groups)
            value = result(g, l, count).astype(BF16)
            for i in range(count):
                ret_out[j - 1, l + i] = value[:, i * width:(i + 1) * width]
            rows = pl.ds(l, count)
            returns.append((j, cut, send(ret_out.at[j - 1, rows], ret_in.at[j - 1, rows], (g, r))))
    for cut in cuts:
        l, count = row_of(m, cut), cut[2]
        value = result(m, l, count)
        for i in range(count):
            place(m * patch + l + i, value[:, i * width:(i + 1) * width])
    for j, cut, copy in returns:
        copy.wait_recv()
        g = lax.rem(m + groups - j, groups)
        l = row_of(g, cut)
        for i in range(cut[2]):
            place(g * patch + l + i, ret_in[j - 1, l + i].astype(F32))
    for copy in copies:
        copy.wait_send()


def on_device(groups, regions, members, diffusivity, advection, obs_value, obs_rinv, obs_cell, obs_count, loc_index):
    local, lines, width = members.shape
    slots = obs_cell.shape[-1]
    patch = lines // groups
    total = groups * local
    partners = groups - 1
    count = 8 + partners + 3 * partners + 2 * partners + 2 + 4 * partners + 4 * partners
    vmem = pl.BlockSpec(memory_space=pltpu.VMEM)
    flops = 2 * total * total * (3 * slots + 2 * total + patch * width)
    result = pl.pallas_call(
        functools.partial(kernel, groups, regions),
        out_shape=jax.ShapeDtypeStruct((local * lines, width), F32),
        in_specs=[pl.BlockSpec(memory_space=pl.ANY)] + [vmem] * 7,
        out_specs=vmem,
        scratch_shapes=[
            pltpu.VMEM((lines + 2 * STEPS, local, width), BF16),
            pltpu.VMEM((lines + 2 * STEPS, local, width), F32),
            pltpu.VMEM((lines + 2 * STEPS, local, width), F32),
            pltpu.VMEM((lines, local, width), BF16),
            pltpu.VMEM((patch, total, width), BF16),
            pltpu.VMEM((4, lines + 16, width), F32),
            pltpu.VMEM((2, 2, 8, width), F32),
            pltpu.VMEM((8, slots), jnp.int32),
            pltpu.VMEM((partners, 8, slots), jnp.int32),
            pltpu.VMEM((8, slots), F32),
            pltpu.VMEM((2, 8, slots), F32),
            pltpu.VMEM((partners, local, slots), BF16),
            pltpu.VMEM((3, total, slots), BF16),
            pltpu.VMEM((total, total), BF16),
            pltpu.VMEM((total, patch * width), BF16),
            pltpu.VMEM((8, patch * width), F32),
            pltpu.VMEM((partners, patch, local, width), BF16),
            pltpu.VMEM((partners, patch, local, width), BF16),
            pltpu.SemaphoreType.DMA((1,)),
            pltpu.SemaphoreType.DMA((count,)),
            pltpu.SemaphoreType.DMA((count,)),
        ],
        compiler_params=pltpu.CompilerParams(
            collective_id=0, has_side_effects=True, vmem_limit_bytes=48 * 1024 * 1024
        ),
        cost_estimate=pl.CostEstimate(flops=flops, bytes_accessed=6 * lines * local * width, transcendentals=0),
    )(
        jnp.transpose(members, (1, 0, 2)), diffusivity, advection, obs_value, obs_rinv,
        obs_cell, obs_count, loc_index,
    )
    return result.reshape(local, lines, width)


def solution(mesh):
    return jax.shard_map(
        functools.partial(on_device, mesh.shape["mem"], mesh.shape["reg"]),
        mesh=mesh,
        in_specs=(
            P("mem", "reg", None),
            P("reg", None),
            P("reg", None),
            P("reg", "mem", None),
            P("reg", "mem", None),
            P("reg", "mem", None),
            P("reg", "mem"),
            P("reg", "mem", None),
        ),
        out_specs=P("mem", "reg", None),
        check_vma=False,
    )
```

```python
import functools

import jax
import jax.numpy as jnp
from jax import lax
from jax.experimental import pallas as pl
from jax.experimental.pallas import tpu as pltpu
from jax.sharding import PartitionSpec as P

STEPS = 3
MESH = pl.DeviceIdType.MESH
F32 = jnp.float32
BF16 = jnp.bfloat16
MEMBER_BLOCK = 64


def kernel(
    groups, regions,
    mem_ref, dif_ref, adv_ref, val_ref, rinv_ref, cell_ref, cnt_ref, loc_ref,
    out_ref,
    padded, first, second, fc, states, coef, coef_in, cells_out, cells_in,
    info_out, info_in, hsend, hall, wt, xb, xbar, ret_out, ret_in,
    local_sem, send_sem, recv_sem,
):
    lines, local, width = mem_ref.shape
    patch = lines // groups
    slots = hall.shape[2]
    members = groups * local
    halo = STEPS
    m = lax.axis_index("mem")
    r = lax.axis_index("reg")
    up = lax.rem(r + regions - 1, regions)
    down = lax.rem(r + 1, regions)

    barrier = pltpu.get_barrier_semaphore()
    for side in (up, down):
        pl.semaphore_signal(barrier, inc=1, device_id=(m, side), device_id_type=MESH)
    for j in range(1, groups):
        pl.semaphore_signal(barrier, inc=1, device_id=(lax.rem(m + j, groups), r), device_id_type=MESH)
    own_load = pltpu.make_async_copy(mem_ref, padded.at[pl.ds(halo, lines)], local_sem.at[0])
    own_load.start()
    cells_out[...] = jnp.broadcast_to(cell_ref[0], cells_out.shape)
    slot = lax.broadcasted_iota(jnp.int32, (1, slots), 1)
    own_prec = jnp.where(slot < cnt_ref[...], rinv_ref[0], 0.0)
    reach = (loc_ref[0].astype(F32) + 1.0) * 0.25
    far_prec = (own_prec * jnp.exp(-(reach * reach))).astype(BF16).astype(F32)
    own_val = val_ref[0].astype(F32)
    info_row = lax.broadcasted_iota(jnp.int32, info_out.shape, 0)
    info_out[...] = jnp.where(info_row == 0, own_val, far_prec)
    def put_coef(base, d, a):
        rows = pl.ds(base, d.shape[0])
        coef[0, rows] = 1.0 - 4.0 * d
        coef[1, rows] = d + 0.5 * a
        coef[2, rows] = d - 0.5 * a
        coef[3, rows] = d

    put_coef(8, dif_ref[...], adv_ref[...])

    def step(src, dst, shift, low, high):
        def body(p, _):
            k = [coef[i, pl.ds(p + 8 - halo, 1), :] for i in range(4)]
            for at in range(0, local, MEMBER_BLOCK):
                block = pl.ds(at, MEMBER_BLOCK)
                c = src[p, block, :].astype(F32)
                n = src[p - 1, block, :].astype(F32)
                s = src[p + 1, block, :].astype(F32)
                sides = pltpu.roll(c, width - 1, 1) + pltpu.roll(c, 1, 1)
                value = k[0] * c + k[1] * n + k[2] * s + k[3] * sides
                dst[p - shift, block, :] = value.astype(dst.dtype)
            return 0

        lax.fori_loop(low, high, body, 0)

    own_load.wait()

    def early_at(g):
        return halo * (1 - (g + groups - 1) // groups)

    def late_at(g):
        return (patch - halo) * ((g + groups - 1) // groups)

    early = patch - halo

    def interior_first(g):
        low = g * patch + early_at(g) + halo
        step(padded, first, 0, low - 2, low + early + 2)

    def interior_rest(g):
        low = g * patch + early_at(g) + halo
        high = low + early
        step(first, second, 0, low - 1, high + 1)
        step(second, fc, halo, low, high)

    def edge(g):
        inner = (g + groups - 1) // groups
        end = g * patch + patch
        for s, (src, dst, shift) in enumerate(((padded, first, 0), (first, second, 0), (second, fc, halo))):
            low = (s - 2) * (1 - inner) + (end - 1 - s) * inner + halo
            step(src, dst, shift, low, low + halo)

    for j in range(1, groups):
        interior_first(lax.rem(m + j, groups))

    pl.semaphore_wait(barrier, groups + 1)

    copies = []

    def send(src, dst, target):
        at = len(copies)
        copy = pltpu.make_async_remote_copy(
            src_ref=src, dst_ref=dst, send_sem=send_sem.at[at], recv_sem=recv_sem.at[at],
            device_id=target, device_id_type=MESH,
        )
        copy.start()
        copies.append(copy)
        return copy

    above, below = (m, up), (m, down)
    halo_top = send(mem_ref.at[pl.ds(lines - halo, halo)], padded.at[pl.ds(0, halo)], below)
    halo_bottom = send(mem_ref.at[pl.ds(0, halo)], padded.at[pl.ds(lines + halo, halo)], above)
    coef_top = [
        send(ref.at[pl.ds(lines - 8, 8)], coef_in.at[0, i], below)
        for i, ref in enumerate((dif_ref, adv_ref))
    ]
    coef_bottom = [
        send(ref.at[pl.ds(0, 8)], coef_in.at[1, i], above)
        for i, ref in enumerate((dif_ref, adv_ref))
    ]
    cell_copies = [
        send(cells_out, cells_in.at[j - 1], (lax.rem(m + j, groups), r)) for j in range(1, groups)
    ]
    info_copies = [
        send(info_out, info_in.at[0], below),
        send(info_out, info_in.at[1], above),
    ]

    forwards = []

    def forward(j, late, at, count):
        g = lax.rem(m + j, groups)
        at = at + (late_at(g) if late else early_at(g))
        forwards.append((late, send(
            fc.at[pl.ds(g * patch + at, count)],
            states.at[pl.ds(at, count), pl.ds(m * local, local)],
            (g, r),
        )))

    for j in range(1, groups):
        interior_rest(lax.rem(m + j, groups))
        forward(j, False, 0, early - 1)
    interior_first(m)
    interior_rest(m)

    halo_top.wait_recv()
    halo_bottom.wait_recv()
    for copy in coef_top + coef_bottom:
        copy.wait_recv()
    put_coef(0, coef_in[0, 0], coef_in[0, 1])
    put_coef(lines + 8, coef_in[1, 0], coef_in[1, 1])

    cell_index = lax.broadcasted_iota(jnp.int32, (patch * width, slots), 0)

    def observe(g, cells):
        flat = jnp.concatenate([fc[g * patch + l] for l in range(patch)], axis=1)
        pick = jnp.where(cell_index == cells, 1.0, 0.0).astype(BF16)
        return jnp.dot(flat, pick, preferred_element_type=F32).astype(BF16)

    hx = []
    for j in range(1, groups):
        g = lax.rem(m + j, groups)
        edge(g)
        cell_copies[groups - j - 1].wait_recv()
        hsend[j - 1] = observe(g, cells_in[groups - j - 1, 0:1, :])
        hx.append(send(hsend.at[j - 1], hall.at[0, pl.ds(m * local, local)], (g, r)))
        forward(j, False, early - 1, 1)
    own_rows = pl.ds(pl.multiple_of(m * local, local), local)
    edge(m)
    hall[0, own_rows, :] = observe(m, cell_ref[0])

    def relay(block):
        rows = pl.ds(block * local, local)
        return [
            send(hall.at[0, rows], hall.at[1, rows], below),
            send(hall.at[0, rows], hall.at[2, rows], above),
        ]

    relays = relay(m)
    for l in range(patch):
        states[l, own_rows, :] = fc[m * patch + l]
    for j in range(1, groups):
        hx[j - 1].wait_recv()
        relays += relay(lax.rem(m + groups - j, groups))
        forward(j, True, 0, halo)

    row_id = lax.broadcasted_iota(jnp.int32, (members, members), 0)
    col_id = lax.broadcasted_iota(jnp.int32, (members, members), 1)
    eye = jnp.where(row_id == col_id, 1.0, 0.0)

    def gram(h, value, prec):
        h = h.astype(F32)
        hbar = jnp.sum(h, axis=0, keepdims=True) * (1.0 / members)
        y = h - hbar
        weighted = y * prec
        part = lax.dot_general(
            weighted.astype(BF16), y.astype(BF16), (((1,), (1,)), ((), ())),
            preferred_element_type=F32,
        )
        return part, jnp.sum(weighted * (value - hbar), axis=1, keepdims=True)

    system, force = gram(hall[0], own_val, own_prec)
    system = system + (members - 1.0) * eye

    def perturb(low, count):
        for i in range(count):
            lane = pl.ds(pl.multiple_of((low + i) * width, width), width)
            x = states[low + i].astype(F32)
            mean = jnp.sum(x, axis=0, keepdims=True) * (1.0 / members)
            xbar[0:1, lane] = mean
            xb[:, lane] = (x - mean).astype(BF16)

    for late, copy in forwards[:groups - 1]:
        copy.wait_recv()
    perturb(early_at(m), early - 1)
    for copy in info_copies + relays:
        copy.wait_recv()
    for side in range(2):
        part, more = gram(hall[1 + side], info_in[side, 0:1, :], info_in[side, 1:2, :])
        system, force = system + part, force + more
    total = jnp.sum(jnp.sum(system * system, axis=0, keepdims=True), axis=1, keepdims=True)
    inv_scale = lax.rsqrt(total)
    y1 = system * inv_scale
    y1b = y1.astype(BF16)
    y2 = jnp.dot(y1b, y1b, preferred_element_type=F32)
    tail = (0.0625 * y2 - 0.5625 * y1).astype(BF16)
    z = 2.25 * eye - 2.4375 * y1 + 1.6875 * y2 + jnp.dot(
        y2.astype(BF16), tail, preferred_element_type=F32
    )
    half = jnp.sum(z * force, axis=0, keepdims=True)
    mean_col = jnp.sum(z * half, axis=1, keepdims=True) * inv_scale
    mean_row = jnp.sum(eye * mean_col, axis=0, keepdims=True)
    wt[...] = (jnp.sqrt((members - 1.0) * inv_scale) * z + mean_row).astype(BF16)

    def result(g, l, count):
        lane = pl.ds(pl.multiple_of(l * width, width), count * width)
        rows = pl.ds(pl.multiple_of(g * local, local), local)
        return xbar[0:1, lane] + jnp.dot(wt[rows, :], xb[:, lane], preferred_element_type=F32)

    cuts = ((False, 0, early - 3), (False, early - 3, 2), (False, early - 1, 1), (True, 0, halo))

    def row_of(g, cut):
        return cut[1] + (late_at(g) if cut[0] else early_at(g))

    def place(line, value):
        out_ref[pl.ds(line, local, stride=lines), :] = value

    returns = []
    for cut in cuts:
        l, count = row_of(m, cut), cut[2]
        if cut[0]:
            for late, copy in forwards[groups - 1:]:
                if late:
                    copy.wait_recv()
            perturb(late_at(m), halo)
        elif cut[1] == early - 1:
            for late, copy in forwards[groups - 1:]:
                if not late:
                    copy.wait_recv()
            perturb(l, 1)
        for j in range(1, groups):
            g = lax.rem(m + j, groups)
            value = result(g, l, count).astype(BF16)
            for i in range(count):
                ret_out[j - 1, l + i] = value[:, i * width:(i + 1) * width]
            rows = pl.ds(l, count)
            returns.append((j, cut, send(ret_out.at[j - 1, rows], ret_in.at[j - 1, rows], (g, r))))
    for cut in cuts:
        l, count = row_of(m, cut), cut[2]
        value = result(m, l, count)
        for i in range(count):
            place(m * patch + l + i, value[:, i * width:(i + 1) * width])
    for j, cut, copy in returns:
        copy.wait_recv()
        g = lax.rem(m + groups - j, groups)
        l = row_of(g, cut)
        for i in range(cut[2]):
            place(g * patch + l + i, ret_in[j - 1, l + i].astype(F32))
    for copy in copies:
        copy.wait_send()


def on_device(groups, regions, members, diffusivity, advection, obs_value, obs_rinv, obs_cell, obs_count, loc_index):
    local, lines, width = members.shape
    slots = obs_cell.shape[-1]
    patch = lines // groups
    total = groups * local
    partners = groups - 1
    count = 8 + partners + 3 * partners + partners + 2 * groups + 4 * partners
    vmem = pl.BlockSpec(memory_space=pltpu.VMEM)
    flops = 2 * total * total * (3 * slots + 2 * total + patch * width)
    result = pl.pallas_call(
        functools.partial(kernel, groups, regions),
        out_shape=jax.ShapeDtypeStruct((local * lines, width), F32),
        in_specs=[pl.BlockSpec(memory_space=pl.ANY)] + [vmem] * 7,
        out_specs=vmem,
        scratch_shapes=[
            pltpu.VMEM((lines + 2 * STEPS, local, width), BF16),
            pltpu.VMEM((lines + 2 * STEPS, local, width), F32),
            pltpu.VMEM((lines + 2 * STEPS, local, width), F32),
            pltpu.VMEM((lines, local, width), BF16),
            pltpu.VMEM((patch, total, width), BF16),
            pltpu.VMEM((4, lines + 16, width), F32),
            pltpu.VMEM((2, 2, 8, width), F32),
            pltpu.VMEM((8, slots), jnp.int32),
            pltpu.VMEM((partners, 8, slots), jnp.int32),
            pltpu.VMEM((8, slots), F32),
            pltpu.VMEM((2, 8, slots), F32),
            pltpu.VMEM((partners, local, slots), BF16),
            pltpu.VMEM((3, total, slots), BF16),
            pltpu.VMEM((total, total), BF16),
            pltpu.VMEM((total, patch * width), BF16),
            pltpu.VMEM((8, patch * width), F32),
            pltpu.VMEM((partners, patch, local, width), BF16),
            pltpu.VMEM((partners, patch, local, width), BF16),
            pltpu.SemaphoreType.DMA((1,)),
            pltpu.SemaphoreType.DMA((count,)),
            pltpu.SemaphoreType.DMA((count,)),
        ],
        compiler_params=pltpu.CompilerParams(
            collective_id=0, has_side_effects=True, vmem_limit_bytes=48 * 1024 * 1024
        ),
        cost_estimate=pl.CostEstimate(flops=flops, bytes_accessed=6 * lines * local * width, transcendentals=0),
    )(
        jnp.transpose(members, (1, 0, 2)), diffusivity, advection, obs_value, obs_rinv,
        obs_cell, obs_count, loc_index,
    )
    return result.reshape(local, lines, width)


def solution(mesh):
    return jax.shard_map(
        functools.partial(on_device, mesh.shape["mem"], mesh.shape["reg"]),
        mesh=mesh,
        in_specs=(
            P("mem", "reg", None),
            P("reg", None),
            P("reg", None),
            P("reg", "mem", None),
            P("reg", "mem", None),
            P("reg", "mem", None),
            P("reg", "mem"),
            P("reg", "mem", None),
        ),
        out_specs=P("mem", "reg", None),
        check_vma=False,
    )
```

```python
import functools

import jax
import jax.numpy as jnp
from jax import lax
from jax.experimental import pallas as pl
from jax.experimental.pallas import tpu as pltpu
from jax.sharding import PartitionSpec as P

STEPS = 3
MESH = pl.DeviceIdType.MESH
F32 = jnp.float32
BF16 = jnp.bfloat16
MEMBER_BLOCK = 64


def kernel(
    groups, regions,
    mem_ref, dif_ref, adv_ref, val_ref, rinv_ref, cell_ref, cnt_ref, loc_ref,
    out_ref,
    padded, first, second, fc, states, coef, coef_in, cells_out, cells_in,
    info_out, info_in, hsend, hall, wt, xb, xbar, ret_out, ret_in,
    local_sem, send_sem, recv_sem,
):
    lines, local, width = mem_ref.shape
    patch = lines // groups
    slots = hall.shape[2]
    members = groups * local
    halo = STEPS
    m = lax.axis_index("mem")
    r = lax.axis_index("reg")
    up = lax.rem(r + regions - 1, regions)
    down = lax.rem(r + 1, regions)

    barrier = pltpu.get_barrier_semaphore()
    for side in (up, down):
        pl.semaphore_signal(barrier, inc=1, device_id=(m, side), device_id_type=MESH)
    for j in range(1, groups):
        pl.semaphore_signal(barrier, inc=1, device_id=(lax.rem(m + j, groups), r), device_id_type=MESH)
    own_load = pltpu.make_async_copy(mem_ref, padded.at[pl.ds(halo, lines)], local_sem.at[0])
    own_load.start()
    cells_out[...] = jnp.broadcast_to(cell_ref[0], cells_out.shape)
    slot = lax.broadcasted_iota(jnp.int32, (1, slots), 1)
    own_prec = jnp.where(slot < cnt_ref[...], rinv_ref[0], 0.0)
    reach = (loc_ref[0].astype(F32) + 1.0) * 0.25
    far_prec = (own_prec * jnp.exp(-(reach * reach))).astype(BF16).astype(F32)
    own_val = val_ref[0].astype(F32)
    info_row = lax.broadcasted_iota(jnp.int32, info_out.shape, 0)
    info_out[...] = jnp.where(info_row == 0, own_val, far_prec)
    def put_coef(base, d, a):
        rows = pl.ds(base, d.shape[0])
        coef[0, rows] = 1.0 - 4.0 * d
        coef[1, rows] = d + 0.5 * a
        coef[2, rows] = d - 0.5 * a
        coef[3, rows] = d

    put_coef(8, dif_ref[...], adv_ref[...])

    def step(src, dst, shift, low, high):
        def body(p, _):
            k = [coef[i, pl.ds(p + 8 - halo, 1), :] for i in range(4)]
            for at in range(0, local, MEMBER_BLOCK):
                block = pl.ds(at, MEMBER_BLOCK)
                c = src[p, block, :].astype(F32)
                n = src[p - 1, block, :].astype(F32)
                s = src[p + 1, block, :].astype(F32)
                sides = pltpu.roll(c, width - 1, 1) + pltpu.roll(c, 1, 1)
                value = k[0] * c + k[1] * n + k[2] * s + k[3] * sides
                dst[p - shift, block, :] = value.astype(dst.dtype)
            return 0

        lax.fori_loop(low, high, body, 0)

    own_load.wait()

    def early_at(g):
        return halo * (1 - (g + groups - 1) // groups)

    def late_at(g):
        return (patch - halo) * ((g + groups - 1) // groups)

    early = patch - halo

    def interior(g):
        low = g * patch + early_at(g) + halo
        high = low + early
        step(padded, first, 0, low - 2, high + 2)
        step(first, second, 0, low - 1, high + 1)
        step(second, fc, halo, low, high)

    def edge(g):
        inner = (g + groups - 1) // groups
        end = g * patch + patch
        for s, (src, dst, shift) in enumerate(((padded, first, 0), (first, second, 0), (second, fc, halo))):
            low = (s - 2) * (1 - inner) + (end - 1 - s) * inner + halo
            step(src, dst, shift, low, low + halo)

    for j in range(1, groups):
        interior(lax.rem(m + j, groups))

    pl.semaphore_wait(barrier, groups + 1)

    copies = []

    def send(src, dst, target):
        at = len(copies)
        copy = pltpu.make_async_remote_copy(
            src_ref=src, dst_ref=dst, send_sem=send_sem.at[at], recv_sem=recv_sem.at[at],
            device_id=target, device_id_type=MESH,
        )
        copy.start()
        copies.append(copy)
        return copy

    above, below = (m, up), (m, down)
    halo_top = send(mem_ref.at[pl.ds(lines - halo, halo)], padded.at[pl.ds(0, halo)], below)
    halo_bottom = send(mem_ref.at[pl.ds(0, halo)], padded.at[pl.ds(lines + halo, halo)], above)
    coef_top = [
        send(ref.at[pl.ds(lines - 8, 8)], coef_in.at[0, i], below)
        for i, ref in enumerate((dif_ref, adv_ref))
    ]
    coef_bottom = [
        send(ref.at[pl.ds(0, 8)], coef_in.at[1, i], above)
        for i, ref in enumerate((dif_ref, adv_ref))
    ]
    cell_copies = [
        send(cells_out, cells_in.at[j - 1], (lax.rem(m + j, groups), r)) for j in range(1, groups)
    ]
    info_copies = [
        send(info_out, info_in.at[0], below),
        send(info_out, info_in.at[1], above),
    ]

    forwards = []

    def forward(j, late, at, count):
        g = lax.rem(m + j, groups)
        at = at + (late_at(g) if late else early_at(g))
        forwards.append((late, send(
            fc.at[pl.ds(g * patch + at, count)],
            states.at[pl.ds(at, count), pl.ds(m * local, local)],
            (g, r),
        )))

    for j in range(1, groups):
        forward(j, False, 0, early - 1)
    interior(m)

    halo_top.wait_recv()
    halo_bottom.wait_recv()
    for copy in coef_top + coef_bottom:
        copy.wait_recv()
    put_coef(0, coef_in[0, 0], coef_in[0, 1])
    put_coef(lines + 8, coef_in[1, 0], coef_in[1, 1])

    cell_index = lax.broadcasted_iota(jnp.int32, (patch * width, slots), 0)

    def observe(g, cells):
        flat = jnp.concatenate([fc[g * patch + l] for l in range(patch)], axis=1)
        pick = jnp.where(cell_index == cells, 1.0, 0.0).astype(BF16)
        return jnp.dot(flat, pick, preferred_element_type=F32).astype(BF16)

    hx = []
    for j in range(1, groups):
        g = lax.rem(m + j, groups)
        edge(g)
        cell_copies[groups - j - 1].wait_recv()
        hsend[j - 1] = observe(g, cells_in[groups - j - 1, 0:1, :])
        hx.append(send(hsend.at[j - 1], hall.at[0, pl.ds(m * local, local)], (g, r)))
        forward(j, False, early - 1, 1)
    own_rows = pl.ds(pl.multiple_of(m * local, local), local)
    edge(m)
    hall[0, own_rows, :] = observe(m, cell_ref[0])

    def relay(block):
        rows = pl.ds(block * local, local)
        return [
            send(hall.at[0, rows], hall.at[1, rows], below),
            send(hall.at[0, rows], hall.at[2, rows], above),
        ]

    relays = relay(m)
    for l in range(patch):
        states[l, own_rows, :] = fc[m * patch + l]
    for j in range(1, groups):
        hx[j - 1].wait_recv()
        relays += relay(lax.rem(m + groups - j, groups))
        forward(j, True, 0, halo)

    row_id = lax.broadcasted_iota(jnp.int32, (members, members), 0)
    col_id = lax.broadcasted_iota(jnp.int32, (members, members), 1)
    eye = jnp.where(row_id == col_id, 1.0, 0.0)

    def gram(h, value, prec):
        h = h.astype(F32)
        hbar = jnp.sum(h, axis=0, keepdims=True) * (1.0 / members)
        y = h - hbar
        weighted = y * prec
        part = lax.dot_general(
            weighted.astype(BF16), y.astype(BF16), (((1,), (1,)), ((), ())),
            preferred_element_type=F32,
        )
        return part, jnp.sum(weighted * (value - hbar), axis=1, keepdims=True)

    system, force = gram(hall[0], own_val, own_prec)
    system = system + (members - 1.0) * eye

    def perturb(low, count):
        for i in range(count):
            lane = pl.ds(pl.multiple_of((low + i) * width, width), width)
            x = states[low + i].astype(F32)
            mean = jnp.sum(x, axis=0, keepdims=True) * (1.0 / members)
            xbar[0:1, lane] = mean
            xb[:, lane] = (x - mean).astype(BF16)

    for late, copy in forwards[:groups - 1]:
        copy.wait_recv()
    perturb(early_at(m), early - 1)
    for side in range(2):
        for copy in [info_copies[side]] + relays[side::2]:
            copy.wait_recv()
        part, more = gram(hall[1 + side], info_in[side, 0:1, :], info_in[side, 1:2, :])
        system, force = system + part, force + more
    total = jnp.sum(jnp.sum(system * system, axis=0, keepdims=True), axis=1, keepdims=True)
    inv_scale = lax.rsqrt(total)
    y1 = system * inv_scale
    y1b = y1.astype(BF16)
    y2 = jnp.dot(y1b, y1b, preferred_element_type=F32)
    tail = (0.0625 * y2 - 0.5625 * y1).astype(BF16)
    z = 2.25 * eye - 2.4375 * y1 + 1.6875 * y2 + jnp.dot(
        y2.astype(BF16), tail, preferred_element_type=F32
    )
    half = jnp.sum(z * force, axis=0, keepdims=True)
    mean_col = jnp.sum(z * half, axis=1, keepdims=True) * inv_scale
    mean_row = jnp.sum(eye * mean_col, axis=0, keepdims=True)
    wt[...] = (jnp.sqrt((members - 1.0) * inv_scale) * z + mean_row).astype(BF16)

    def result(g, l, count):
        lane = pl.ds(pl.multiple_of(l * width, width), count * width)
        rows = pl.ds(pl.multiple_of(g * local, local), local)
        return xbar[0:1, lane] + jnp.dot(wt[rows, :], xb[:, lane], preferred_element_type=F32)

    cuts = ((False, 0, early - 3), (False, early - 3, 2), (False, early - 1, 1), (True, 0, halo))

    def row_of(g, cut):
        return cut[1] + (late_at(g) if cut[0] else early_at(g))

    def place(line, value):
        out_ref[pl.ds(line, local, stride=lines), :] = value

    returns = []
    for cut in cuts:
        l, count = row_of(m, cut), cut[2]
        if cut[0]:
            for late, copy in forwards[groups - 1:]:
                if late:
                    copy.wait_recv()
            perturb(late_at(m), halo)
        elif cut[1] == early - 1:
            for late, copy in forwards[groups - 1:]:
                if not late:
                    copy.wait_recv()
            perturb(l, 1)
        for j in range(1, groups):
            g = lax.rem(m + j, groups)
            value = result(g, l, count).astype(BF16)
            for i in range(count):
                ret_out[j - 1, l + i] = value[:, i * width:(i + 1) * width]
            rows = pl.ds(l, count)
            returns.append((j, cut, send(ret_out.at[j - 1, rows], ret_in.at[j - 1, rows], (g, r))))
    for cut in cuts:
        l, count = row_of(m, cut), cut[2]
        value = result(m, l, count)
        for i in range(count):
            place(m * patch + l + i, value[:, i * width:(i + 1) * width])
    for j, cut, copy in returns:
        copy.wait_recv()
        g = lax.rem(m + groups - j, groups)
        l = row_of(g, cut)
        for i in range(cut[2]):
            place(g * patch + l + i, ret_in[j - 1, l + i].astype(F32))
    for copy in copies:
        copy.wait_send()


def on_device(groups, regions, members, diffusivity, advection, obs_value, obs_rinv, obs_cell, obs_count, loc_index):
    local, lines, width = members.shape
    slots = obs_cell.shape[-1]
    patch = lines // groups
    total = groups * local
    partners = groups - 1
    count = 8 + partners + 3 * partners + partners + 2 * groups + 4 * partners
    vmem = pl.BlockSpec(memory_space=pltpu.VMEM)
    flops = 2 * total * total * (3 * slots + 2 * total + patch * width)
    result = pl.pallas_call(
        functools.partial(kernel, groups, regions),
        out_shape=jax.ShapeDtypeStruct((local * lines, width), F32),
        in_specs=[pl.BlockSpec(memory_space=pl.ANY)] + [vmem] * 7,
        out_specs=vmem,
        scratch_shapes=[
            pltpu.VMEM((lines + 2 * STEPS, local, width), BF16),
            pltpu.VMEM((lines + 2 * STEPS, local, width), F32),
            pltpu.VMEM((lines + 2 * STEPS, local, width), F32),
            pltpu.VMEM((lines, local, width), BF16),
            pltpu.VMEM((patch, total, width), BF16),
            pltpu.VMEM((4, lines + 16, width), F32),
            pltpu.VMEM((2, 2, 8, width), F32),
            pltpu.VMEM((8, slots), jnp.int32),
            pltpu.VMEM((partners, 8, slots), jnp.int32),
            pltpu.VMEM((8, slots), F32),
            pltpu.VMEM((2, 8, slots), F32),
            pltpu.VMEM((partners, local, slots), BF16),
            pltpu.VMEM((3, total, slots), BF16),
            pltpu.VMEM((total, total), BF16),
            pltpu.VMEM((total, patch * width), BF16),
            pltpu.VMEM((8, patch * width), F32),
            pltpu.VMEM((partners, patch, local, width), BF16),
            pltpu.VMEM((partners, patch, local, width), BF16),
            pltpu.SemaphoreType.DMA((1,)),
            pltpu.SemaphoreType.DMA((count,)),
            pltpu.SemaphoreType.DMA((count,)),
        ],
        compiler_params=pltpu.CompilerParams(
            collective_id=0, has_side_effects=True, vmem_limit_bytes=48 * 1024 * 1024
        ),
        cost_estimate=pl.CostEstimate(flops=flops, bytes_accessed=6 * lines * local * width, transcendentals=0),
    )(
        jnp.transpose(members, (1, 0, 2)), diffusivity, advection, obs_value, obs_rinv,
        obs_cell, obs_count, loc_index,
    )
    return result.reshape(local, lines, width)


def solution(mesh):
    return jax.shard_map(
        functools.partial(on_device, mesh.shape["mem"], mesh.shape["reg"]),
        mesh=mesh,
        in_specs=(
            P("mem", "reg", None),
            P("reg", None),
            P("reg", None),
            P("reg", "mem", None),
            P("reg", "mem", None),
            P("reg", "mem", None),
            P("reg", "mem"),
            P("reg", "mem", None),
        ),
        out_specs=P("mem", "reg", None),
        check_vma=False,
    )
```
